32 devices in a mesh: groups: 2 (over y), seq: 16 (over z, x, core).
Axes of the slice: x: 2, y: 2, z: 4, core: 2. Of those that a mesh axis runs over, the one named last changes fastest.
Arguments:
- inputs: bfloat16 [32768, 512], P(('groups', 'seq')), parts along dimension 0, may hold values from -36 to 36
- norm_gain: float32 [512], replicated, may hold values from 0.5 to 1.5
- dilated_weight: bfloat16 [3, 512, 512], replicated, may hold values from -0.15625 to 0.15625
- local_weight: bfloat16 [5, 512, 512], replicated, may hold values from -0.125 to 0.125
- cotangent: bfloat16 [32768, 512], P(('groups', 'seq')), parts along dimension 0, may hold values from -6 to 6
Outputs:
- block_out: bfloat16 [32768, 512], P(('groups', 'seq')), parts along dimension 0
- input_grad: bfloat16 [32768, 512], P(('groups', 'seq')), parts along dimension 0
- grad_dilated: float32 [3072, 512], P(('groups', 'seq')), parts along dimension 0
- grad_local: float32 [5120, 512], P(('groups', 'seq')), parts along dimension 0
The draws below stay inside these ranges and needn't reach their ends.
There are 2 independent parts, one for each index of `groups`. The reference program is written for one: setup_inputs(seed, part) draws one part's arguments, and reference() takes and returns one part's arrays. A program takes and returns all parts, laid end to end along the dimension named above; an argument that names none is the same for every part. Nothing has to cross between parts.
All inputs are finite; a program needn't handle non-finite values.
Results may differ from the reference program's by a relative error of at most 0.0053.
Values may be sent and summed in bfloat16 or wider, within the bound.
A program may use at most 128 MiB of HBM per device.

```python
import math
import jax
import jax.numpy as jnp
from jax import lax

C = 512
DILATION_BINS = 8192
LENGTH = 16384


def draw_inputs(key, part):
    base_key, row_key, col_key = jax.random.split(jax.random.fold_in(key, 11), 3)
    row_scale = 0.3 * jnp.exp(jax.random.uniform(row_key, (LENGTH, 1), jnp.float32, 0.0, math.log(10.0)))
    col_scale = 0.3 * jnp.exp(jax.random.uniform(col_key, (1, C), jnp.float32, 0.0, math.log(10.0)))
    base = jax.random.normal(base_key, (LENGTH, C), jnp.float32)
    base = jnp.clip(base, -4.0, 4.0)
    return (base * row_scale * col_scale).astype(jnp.bfloat16)


def level_of(own_key, dims, cuts, smallest, largest):
    def one(dim, blocks):
        draws = jax.random.uniform(jax.random.fold_in(jax.random.fold_in(own_key, 6), dim), (blocks,), jnp.float32, smallest / len(cuts), largest / len(cuts))
        return jnp.repeat(jnp.exp(draws), dims[dim] // blocks).reshape((-1,) + (1,) * (len(dims) - dim - 1))

    level = one(*cuts[0])
    for cut in cuts[1:]:
        level = level * one(*cut)
    return level


def bell_draw(rng, dims, spread, most, shards=(), kind=jnp.bfloat16):
    drawn = jax.random.normal(rng, dims, jnp.float32) * spread
    if len(shards) > 0:
        drawn = level_of(rng, dims, shards, -0.22, 0.18) * drawn
    return jnp.clip(drawn, min=-most, max=most).astype(kind)


def setup_inputs(seed: int = 0, part: int = 0) -> dict:
    arg_keys = jax.random.split(jax.random.key(seed), 6)
    part_keys = jax.random.split(jax.random.fold_in(arg_keys[5], part), 6)
    inputs = draw_inputs(jax.random.fold_in(jax.random.fold_in(arg_keys[5], part), 71), part)
    norm_gain = jnp.clip(1.0 + 0.1 * jax.random.normal(arg_keys[1], (C,), jnp.float32), 0.5, 1.5)
    dilated_weight = bell_draw(arg_keys[2], (3, C, C), (3 * C) ** -0.5, 0.15625)
    local_weight = bell_draw(arg_keys[3], (5, C, C), (5 * C) ** -0.5, 0.125)
    cotangent = bell_draw(part_keys[4], (LENGTH, C), 1.0, 6.0, ((0, 16),))
    return {"inputs": inputs, "norm_gain": norm_gain, "dilated_weight": dilated_weight, "local_weight": local_weight, "cotangent": cotangent}


def shifted_sequence_rows(array, offset):
    if offset == 0:
        return array
    zeros = jnp.zeros((abs(offset), array.shape[1]), array.dtype)
    if offset > 0:
        return jnp.concatenate([zeros, array[:-offset]], axis=0)
    return jnp.concatenate([array[-offset:], zeros], axis=0)

def prepare(values, gain):
    meansq = lax.optimization_barrier(jnp.mean(values * values, axis=-1, keepdims=True)) + 1e-06
    return jax.nn.gelu(values * lax.rsqrt(meansq) * gain, approximate=True)

def reference(inputs, norm_gain, dilated_weight, local_weight, cotangent):
    width = inputs.shape[1]
    scale = float(LENGTH) ** (-0.5)
    values = inputs.astype(jnp.float32)
    act_f, pull = jax.vjp(lambda v: prepare(v, norm_gain), values)
    activation_input = act_f.astype(jnp.bfloat16)
    gathered_activation = jnp.concatenate([shifted_sequence_rows(activation_input, DILATION_BINS), activation_input, shifted_sequence_rows(activation_input, -DILATION_BINS)], axis=1)
    mid = jnp.dot(gathered_activation, dilated_weight.reshape(3 * width, width), preferred_element_type=jnp.float32)
    hid_f, gelu_pull = jax.vjp(lambda m: jax.nn.gelu(m, approximate=True), mid)
    hidden = hid_f.astype(jnp.bfloat16)
    hid_all = jnp.concatenate([shifted_sequence_rows(hidden, 2 - j) for j in range(5)], axis=1)
    out = jnp.dot(hid_all, local_weight.reshape(5 * width, width), preferred_element_type=jnp.float32)
    block_out = (values + out).astype(jnp.bfloat16)
    cot_all = jnp.concatenate([shifted_sequence_rows(cotangent, j - 2) for j in range(5)], axis=1)
    local_t = jnp.transpose(local_weight, (0, 2, 1)).reshape(5 * width, width)
    d_hidden = jnp.dot(cot_all, local_t, preferred_element_type=jnp.float32)
    middle_gradient = gelu_pull(d_hidden)[0].astype(jnp.bfloat16)
    grad_local = jnp.dot(hid_all.T, cotangent, preferred_element_type=jnp.float32) * scale
    gathered_middle_grad = jnp.concatenate([shifted_sequence_rows(middle_gradient, -DILATION_BINS), middle_gradient, shifted_sequence_rows(middle_gradient, DILATION_BINS)], axis=1)
    dilated_t = jnp.transpose(dilated_weight, (0, 2, 1)).reshape(3 * width, width)
    d_act = jnp.dot(gathered_middle_grad, dilated_t, preferred_element_type=jnp.float32)
    grad_dilated = jnp.dot(gathered_activation.T, middle_gradient, preferred_element_type=jnp.float32) * scale
    input_grad = (cotangent.astype(jnp.float32) + pull(d_act)[0]).astype(jnp.bfloat16)
    return (block_out, input_grad, grad_dilated, grad_local)
```

```python
import functools
import itertools
import math

import jax
import jax.numpy as jnp
from jax import lax
from jax.experimental import pallas as pl
from jax.experimental.pallas import tpu as pltpu
from jax.sharding import PartitionSpec as P

DILATION_BINS = 8192
MESH = pl.DeviceIdType.MESH
GELU_A = 0.7978845608028654
GELU_B = 0.044715
CHUNK = 128
PAD = 16
F32 = jnp.float32
BF16 = jnp.bfloat16


def from_behind(x, axis, by):
    devices = lax.axis_size(axis)
    pairs = [(i, i + by) for i in range(devices) if 0 <= i + by < devices]
    return lax.ppermute(x, axis, pairs)


def with_halo(block, sides, width):
    for axis, dim in sides:
        count = lax.axis_size(axis)
        forward = [(i, i + 1) for i in range(count - 1)]
        backward = [(target, source) for source, target in forward]
        low = lax.ppermute(
            lax.slice_in_dim(block, block.shape[dim] - width, None, axis=dim), axis, forward
        )
        high = lax.ppermute(lax.slice_in_dim(block, 0, width, axis=dim), axis, backward)
        block = jnp.concatenate([low, block, high], axis=dim)
    return block


def prepare(values, gain):
    meansq = jnp.mean(values * values, axis=-1, keepdims=True) + 1e-06
    return jax.nn.gelu(values * lax.rsqrt(meansq) * gain, approximate=True)


def transposed_term(left, right, scale):
    product = lax.dot_general(
        left, right, (((0,), (0,)), ((), ())), preferred_element_type=jnp.float32
    )
    return product * scale


def on_device(inputs, norm_gain, dilated_weight, local_weight, cotangent):
    sequence_rows, width = inputs.shape
    devices = lax.axis_size("seq")
    dilation_stride = DILATION_BINS // sequence_rows
    scale = 1.0 / math.sqrt(sequence_rows * devices)
    values = inputs.astype(jnp.float32)
    act_f, pull = jax.vjp(lambda v: prepare(v, norm_gain), values)
    activation_input = act_f.astype(jnp.bfloat16)
    earlier = from_behind(activation_input, "seq", dilation_stride)
    later = from_behind(activation_input, "seq", -dilation_stride)
    gathered_activation = jnp.concatenate([earlier, activation_input, later], axis=1)
    mid = jnp.dot(
        gathered_activation,
        dilated_weight.reshape(3 * width, width),
        preferred_element_type=jnp.float32,
    )
    hid_f, gelu_pull = jax.vjp(lambda m: jax.nn.gelu(m, approximate=True), mid)
    hidden = hid_f.astype(jnp.bfloat16)
    padded = with_halo(hidden, (("seq", 0),), 2)
    hid_all = jnp.concatenate([padded[j : j + sequence_rows] for j in range(5)], axis=1)
    out = jnp.dot(
        hid_all, local_weight.reshape(5 * width, width), preferred_element_type=jnp.float32
    )
    block_out = (values + out).astype(jnp.bfloat16)
    cot_padded = with_halo(cotangent, (("seq", 0),), 2)
    cot_all = jnp.concatenate([cot_padded[4 - j : 4 - j + sequence_rows] for j in range(5)], axis=1)
    local_t = jnp.transpose(local_weight, (0, 2, 1)).reshape(5 * width, width)
    d_hidden = jnp.dot(cot_all, local_t, preferred_element_type=jnp.float32)
    middle_gradient = gelu_pull(d_hidden)[0].astype(jnp.bfloat16)
    grad_local = lax.psum_scatter(
        transposed_term(hid_all, cotangent, scale), "seq", scatter_dimension=0, tiled=True
    )
    dilated_t = jnp.transpose(dilated_weight, (0, 2, 1))
    first_part = jnp.dot(middle_gradient, dilated_t[0], preferred_element_type=jnp.float32)
    last_part = jnp.dot(middle_gradient, dilated_t[2], preferred_element_type=jnp.float32)
    centre_part = jnp.dot(middle_gradient, dilated_t[1], preferred_element_type=jnp.float32)
    moved_first = from_behind(first_part.astype(jnp.bfloat16), "seq", -dilation_stride).astype(
        first_part.dtype
    )
    moved_last = from_behind(last_part.astype(jnp.bfloat16), "seq", dilation_stride).astype(
        last_part.dtype
    )
    d_act = moved_first + centre_part + moved_last
    grad_dilated = lax.psum_scatter(
        transposed_term(gathered_activation, middle_gradient, scale),
        "seq",
        scatter_dimension=0,
        tiled=True,
    )
    input_grad = (cotangent.astype(jnp.float32) + pull(d_act)[0]).astype(jnp.bfloat16)
    return (block_out, input_grad, grad_dilated, grad_local)


def gelu_and_slope(u):
    t = jnp.tanh(GELU_A * (u + GELU_B * (u * u * u)))
    half = 0.5 * (1.0 + t)
    slope = half + 0.5 * u * (1.0 - t * t) * (GELU_A * (1.0 + 3.0 * GELU_B * (u * u)))
    return u * half, slope


def dot(x, w):
    return jnp.dot(x, w, preferred_element_type=F32)


def dot_t(x, w):
    return lax.dot_general(x, w, (((1,), (1,)), ((), ())), preferred_element_type=F32)


def bit_of(index, bit):
    return lax.rem(lax.div(index, bit), 2)


def across(index, bit):
    return index + bit - 2 * bit * bit_of(index, bit)


class HalvingSum:
    def __init__(self, me, order, rows, acc, stage, recv, out, send_sem, recv_sem, scale):
        self.me, self.order, self.rows, self.acc = me, order, rows, acc
        self.stage, self.recv, self.out = stage, recv, out
        self.send_sem, self.recv_sem, self.scale = send_sem, recv_sem, scale
        self.base = [0]
        for k in range(len(order)):
            self.base.append(self.base[-1] + 2 ** (len(order) - 1 - k))

    def combos(self, k):
        return list(itertools.product((1, 0), repeat=len(self.order) - 1 - k))

    def copy(self, k, slot):
        s = self.base[k] + slot
        return pltpu.make_async_remote_copy(
            src_ref=self.stage.at[s],
            dst_ref=self.recv.at[s],
            send_sem=self.send_sem.at[s],
            recv_sem=self.recv_sem.at[s],
            device_id={"seq": across(self.me, self.order[k])},
            device_id_type=MESH,
        )

    def block(self, flips):
        index = 0
        for bit, flip in zip(self.order, flips):
            mine = bit_of(self.me, bit)
            index = index + bit * (1 - mine if flip else mine)
        return pl.ds(pl.multiple_of(index * self.rows, 16), self.rows)

    def begin(self):
        for slot, rel in enumerate(self.combos(0)):
            self.stage[slot] = self.acc[self.block((1,) + rel), :].astype(BF16)
            self.copy(0, slot).start()

    def step(self, k):
        for slot, rel in enumerate(self.combos(k)):
            self.copy(k, slot).wait_recv()
            block = self.block((0,) * (k + 1) + rel)
            total = self.acc[block, :] + self.recv[self.base[k] + slot].astype(F32)
            if not rel:
                self.out[...] = total * self.scale
            elif rel[0]:
                later = self.combos(k + 1).index(rel[1:])
                self.stage[self.base[k + 1] + later] = total.astype(BF16)
                self.copy(k + 1, later).start()
            else:
                self.acc[block, :] = total

    def finish(self):
        for k in range(len(self.order)):
            for slot in range(len(self.combos(k))):
                self.copy(k, slot).wait_send()


def fused_kernel(
    devices, stride, scale,
    x_ref, gain_ref, dw_ref, lw_ref, cot_ref,
    bo_ref, ig_ref, gd_ref, gl_ref,
    act, act_in, act_t, act_in_t, cotp, hidp, cots, d_hid, slope_in, hid_t, dmid, dmid_in,
    acc_l, acc_d, stage_l, recv_l, stage_d, recv_d,
    act_ss, act_rs, dm_ss, dm_rs, halo_ss, halo_rs, l_ss, l_rs, d_ss, d_rs,
):
    rows, width = x_ref.shape
    chunks = rows // CHUNK
    me = lax.axis_index("seq")
    upper = lax.div(me, stride)
    far = across(me, stride)
    tap_in = 2 - 2 * upper
    tap_out = 2 * upper
    has_left, has_right = me > 0, me < devices - 1
    left, right = jnp.maximum(me - 1, 0), jnp.minimum(me + 1, devices - 1)
    bits = [1 << i for i in range(devices.bit_length() - 1)]

    barrier = pltpu.get_barrier_semaphore()
    for bit in bits:
        pl.semaphore_signal(barrier, inc=1, device_id={"seq": across(me, bit)}, device_id_type=MESH)

    @pl.when(has_left)
    def _():
        pl.semaphore_signal(barrier, inc=1, device_id={"seq": left}, device_id_type=MESH)

    @pl.when(has_right)
    def _():
        pl.semaphore_signal(barrier, inc=1, device_id={"seq": right}, device_id_type=MESH)

    def chunk(c):
        return pl.ds(pl.multiple_of(c * CHUNK, CHUNK), CHUNK)

    def padded_chunk(c):
        return pl.ds(pl.multiple_of(PAD + c * CHUNK, PAD), CHUNK)

    def moved(src, dst, ss, rs, c):
        return pltpu.make_async_remote_copy(
            src_ref=src.at[chunk(c)], dst_ref=dst.at[chunk(c)],
            send_sem=ss.at[c], recv_sem=rs.at[c],
            device_id={"seq": far}, device_id_type=MESH,
        )

    def to_right(buf, k):
        return pltpu.make_async_remote_copy(
            src_ref=buf.at[pl.ds(rows, PAD)], dst_ref=buf.at[pl.ds(0, PAD)],
            send_sem=halo_ss.at[k], recv_sem=halo_rs.at[k],
            device_id={"seq": right}, device_id_type=MESH,
        )

    def to_left(buf, k):
        return pltpu.make_async_remote_copy(
            src_ref=buf.at[pl.ds(PAD, PAD)], dst_ref=buf.at[pl.ds(rows + PAD, PAD)],
            send_sem=halo_ss.at[k], recv_sem=halo_rs.at[k],
            device_id={"seq": left}, device_id_type=MESH,
        )

    def halo_start(buf, k):
        @pl.when(has_right)
        def _():
            to_right(buf, k).start()

        @pl.when(has_left)
        def _():
            to_left(buf, k + 1).start()

    def halo_wait(buf, k):
        @pl.when(has_right)
        def _():
            to_right(buf, k).wait_send()
            to_left(buf, k + 1).wait_recv()

        @pl.when(has_left)
        def _():
            to_left(buf, k + 1).wait_send()
            to_right(buf, k).wait_recv()

    @pl.when(jnp.logical_not(has_left))
    def _():
        cotp[0:PAD, :] = jnp.zeros((PAD, width), BF16)
        hidp[0:PAD, :] = jnp.zeros((PAD, width), BF16)

    @pl.when(jnp.logical_not(has_right))
    def _():
        cotp[rows + PAD : rows + 2 * PAD, :] = jnp.zeros((PAD, width), BF16)
        hidp[rows + PAD : rows + 2 * PAD, :] = jnp.zeros((PAD, width), BF16)

    cotp[PAD : rows + PAD, :] = cot_ref[...]
    pl.semaphore_wait(
        barrier, len(bits) + has_left.astype(jnp.int32) + has_right.astype(jnp.int32)
    )
    halo_start(cotp, 0)

    def prepare_chunk(c, _):
        v = x_ref[chunk(c), :].astype(F32)
        rstd = lax.rsqrt(jnp.mean(v * v, axis=-1, keepdims=True) + 1e-06)
        a, slope = gelu_and_slope(v * rstd * gain_ref[...])
        act[chunk(c), :] = a.astype(BF16)
        moved(act, act_in, act_ss, act_rs, c).start()
        slope_in[chunk(c), :] = slope * gain_ref[...]
        return 0

    lax.fori_loop(0, chunks, prepare_chunk, 0)
    halo_wait(cotp, 0)

    def cot_chunk(c, _):
        window = cotp[pl.ds(pl.multiple_of(c * CHUNK, CHUNK), CHUNK + 2 * PAD), :].astype(F32)
        total = jnp.zeros((CHUNK, width), F32)
        for j in range(5):
            shifted = window[PAD + 2 - j : PAD + 2 - j + CHUNK].astype(BF16)
            cots[j, chunk(c), :] = shifted
            total = total + dot_t(shifted, lw_ref[j])
        d_hid[chunk(c), :] = total
        act_t[:, chunk(c)] = act[chunk(c), :].astype(F32).T.astype(BF16)
        return 0

    lax.fori_loop(0, chunks, cot_chunk, 0)

    def middle_chunk(c, _):
        moved(act, act_in, act_ss, act_rs, c).wait_recv()
        other = act_in[chunk(c), :]
        mid = dot(act[chunk(c), :], dw_ref[1]) + dot(other, dw_ref[tap_in])
        hid, slope = gelu_and_slope(mid)
        dm = (d_hid[chunk(c), :] * slope).astype(BF16)
        dmid[chunk(c), :] = dm
        moved(dmid, dmid_in, dm_ss, dm_rs, c).start()
        hid = hid.astype(BF16)
        hidp[padded_chunk(c), :] = hid
        hid_t[:, chunk(c)] = hid.astype(F32).T.astype(BF16)
        act_in_t[:, chunk(c)] = other.astype(F32).T.astype(BF16)
        return 0

    lax.fori_loop(0, chunks, middle_chunk, 0)
    halo_start(hidp, 2)

    sum_l = HalvingSum(
        me, bits, gl_ref.shape[0], acc_l, stage_l, recv_l, gl_ref, l_ss, l_rs, scale
    )
    d_order = [bits[0], bits[2], bits[1]] + bits[3:]
    sum_d = HalvingSum(
        me, d_order, gd_ref.shape[0], acc_d, stage_d, recv_d, gd_ref, d_ss, d_rs, scale
    )

    def local_tap(j, _):
        acc_l[pl.ds(pl.multiple_of(j * width, width), width), :] = dot(hid_t[...], cots[j])
        return 0

    lax.fori_loop(0, 5, local_tap, 0)
    sum_l.begin()
    acc_d[width : 2 * width, :] = dot(act_t[...], dmid[...])
    acc_d[pl.ds(pl.multiple_of(tap_in * width, width), width), :] = dot(act_in_t[...], dmid[...])
    acc_d[pl.ds(pl.multiple_of(tap_out * width, width), width), :] = jnp.zeros((width, width), F32)
    sum_d.begin()
    sum_l.step(0)
    sum_d.step(0)

    halo_wait(hidp, 2)

    def out_chunk(c, _):
        window = hidp[pl.ds(pl.multiple_of(c * CHUNK, CHUNK), CHUNK + 2 * PAD), :].astype(F32)
        total = x_ref[chunk(c), :].astype(F32)
        for j in range(5):
            total = total + dot(window[PAD - 2 + j : PAD - 2 + j + CHUNK].astype(BF16), lw_ref[j])
        bo_ref[chunk(c), :] = total.astype(BF16)
        return 0

    lax.fori_loop(0, chunks, out_chunk, 0)
    for k in range(1, len(bits) - 1):
        sum_l.step(k)
        sum_d.step(k)

    def grad_chunk(c, _):
        moved(dmid, dmid_in, dm_ss, dm_rs, c).wait_recv()
        d_act = dot_t(dmid[chunk(c), :], dw_ref[1]) + dot_t(dmid_in[chunk(c), :], dw_ref[tap_out])
        v = x_ref[chunk(c), :].astype(F32)
        rstd = lax.rsqrt(jnp.mean(v * v, axis=-1, keepdims=True) + 1e-06)
        du = d_act * slope_in[chunk(c), :]
        unit = v * rstd
        dv = rstd * (du - unit * jnp.mean(du * unit, axis=-1, keepdims=True))
        ig_ref[chunk(c), :] = (cot_ref[chunk(c), :].astype(F32) + dv).astype(BF16)
        return 0

    lax.fori_loop(0, chunks, grad_chunk, 0)
    sum_l.step(len(bits) - 1)
    sum_d.step(len(bits) - 1)

    def sent(c, _):
        moved(act, act_in, act_ss, act_rs, c).wait_send()
        moved(dmid, dmid_in, dm_ss, dm_rs, c).wait_send()
        return 0

    lax.fori_loop(0, chunks, sent, 0)
    sum_l.finish()
    sum_d.finish()


def paired(devices, inputs, norm_gain, dilated_weight, local_weight, cotangent):
    rows, width = inputs.shape
    stride = DILATION_BINS // rows
    scale = 1.0 / math.sqrt(rows * devices)
    chunks = rows // CHUNK
    rows_d, rows_l = 3 * width // devices, 5 * width // devices
    vmem = pltpu.VMEM
    dma = pltpu.SemaphoreType.DMA
    whole = pl.BlockSpec(memory_space=pltpu.VMEM)
    flops = 2 * rows * width * width * (5 * 3 + 2 * 3)
    return pl.pallas_call(
        functools.partial(fused_kernel, devices, stride, scale),
        out_shape=(
            jax.ShapeDtypeStruct((rows, width), BF16),
            jax.ShapeDtypeStruct((rows, width), BF16),
            jax.ShapeDtypeStruct((rows_d, width), F32),
            jax.ShapeDtypeStruct((rows_l, width), F32),
        ),
        in_specs=[whole] * 5,
        out_specs=(whole,) * 4,
        scratch_shapes=[
            vmem((rows, width), BF16),
            vmem((rows, width), BF16),
            vmem((width, rows), BF16),
            vmem((width, rows), BF16),
            vmem((rows + 2 * PAD, width), BF16),
            vmem((rows + 2 * PAD, width), BF16),
            vmem((5, rows, width), BF16),
            vmem((rows, width), F32),
            vmem((rows, width), F32),
            vmem((width, rows), BF16),
            vmem((rows, width), BF16),
            vmem((rows, width), BF16),
            vmem((5 * width, width), F32),
            vmem((3 * width, width), F32),
            vmem((devices - 1, rows_l, width), BF16),
            vmem((devices - 1, rows_l, width), BF16),
            vmem((devices - 1, rows_d, width), BF16),
            vmem((devices - 1, rows_d, width), BF16),
            dma((chunks,)), dma((chunks,)), dma((chunks,)), dma((chunks,)),
            dma((4,)), dma((4,)),
            dma((devices - 1,)), dma((devices - 1,)), dma((devices - 1,)), dma((devices - 1,)),
        ],
        compiler_params=pltpu.CompilerParams(
            collective_id=0, has_side_effects=True, vmem_limit_bytes=58 * 2**20
        ),
        cost_estimate=pl.CostEstimate(
            flops=flops, bytes_accessed=12 * 2**20, transcendentals=2 * rows * width
        ),
    )(inputs, norm_gain.reshape(1, width), dilated_weight, local_weight, cotangent)


def pairs_up(devices, rows, width):
    return (
        devices >= 8
        and devices & (devices - 1) == 0
        and devices * rows == 2 * DILATION_BINS
        and rows % CHUNK == 0
        and width % (16 * devices) == 0
    )


def solution(mesh):
    def body(inputs, norm_gain, dilated_weight, local_weight, cotangent):
        arrays = (inputs, norm_gain, dilated_weight, local_weight, cotangent)
        devices = mesh.shape["seq"]
        if pairs_up(devices, *inputs.shape):
            return paired(devices, *arrays)
        return on_device(*arrays)

    return jax.shard_map(
        body,
        mesh=mesh,
        in_specs=(P(("groups", "seq"), None), P(), P(), P(), P(("groups", "seq"), None)),
        out_specs=(
            P(("groups", "seq"), None),
            P(("groups", "seq"), None),
            P(("groups", "seq"), None),
            P(("groups", "seq"), None),
        ),
        check_vma=False,
    )
```

```python
import functools
import itertools
import math

import jax
import jax.numpy as jnp
from jax import lax
from jax.experimental import pallas as pl
from jax.experimental.pallas import tpu as pltpu
from jax.sharding import PartitionSpec as P

DILATION_BINS = 8192
MESH = pl.DeviceIdType.MESH
GELU_A = 0.7978845608028654
GELU_B = 0.044715
CHUNK = 128
PAD = 16
LAG = 4
F32 = jnp.float32
BF16 = jnp.bfloat16


def from_behind(x, axis, by):
    devices = lax.axis_size(axis)
    pairs = [(i, i + by) for i in range(devices) if 0 <= i + by < devices]
    return lax.ppermute(x, axis, pairs)


def with_halo(block, sides, width):
    for axis, dim in sides:
        count = lax.axis_size(axis)
        forward = [(i, i + 1) for i in range(count - 1)]
        backward = [(target, source) for source, target in forward]
        low = lax.ppermute(
            lax.slice_in_dim(block, block.shape[dim] - width, None, axis=dim), axis, forward
        )
        high = lax.ppermute(lax.slice_in_dim(block, 0, width, axis=dim), axis, backward)
        block = jnp.concatenate([low, block, high], axis=dim)
    return block


def prepare(values, gain):
    meansq = jnp.mean(values * values, axis=-1, keepdims=True) + 1e-06
    return jax.nn.gelu(values * lax.rsqrt(meansq) * gain, approximate=True)


def transposed_term(left, right, scale):
    product = lax.dot_general(
        left, right, (((0,), (0,)), ((), ())), preferred_element_type=jnp.float32
    )
    return product * scale


def on_device(inputs, norm_gain, dilated_weight, local_weight, cotangent):
    sequence_rows, width = inputs.shape
    devices = lax.axis_size("seq")
    dilation_stride = DILATION_BINS // sequence_rows
    scale = 1.0 / math.sqrt(sequence_rows * devices)
    values = inputs.astype(jnp.float32)
    act_f, pull = jax.vjp(lambda v: prepare(v, norm_gain), values)
    activation_input = act_f.astype(jnp.bfloat16)
    earlier = from_behind(activation_input, "seq", dilation_stride)
    later = from_behind(activation_input, "seq", -dilation_stride)
    gathered_activation = jnp.concatenate([earlier, activation_input, later], axis=1)
    mid = jnp.dot(
        gathered_activation,
        dilated_weight.reshape(3 * width, width),
        preferred_element_type=jnp.float32,
    )
    hid_f, gelu_pull = jax.vjp(lambda m: jax.nn.gelu(m, approximate=True), mid)
    hidden = hid_f.astype(jnp.bfloat16)
    padded = with_halo(hidden, (("seq", 0),), 2)
    hid_all = jnp.concatenate([padded[j : j + sequence_rows] for j in range(5)], axis=1)
    out = jnp.dot(
        hid_all, local_weight.reshape(5 * width, width), preferred_element_type=jnp.float32
    )
    block_out = (values + out).astype(jnp.bfloat16)
    cot_padded = with_halo(cotangent, (("seq", 0),), 2)
    cot_all = jnp.concatenate([cot_padded[4 - j : 4 - j + sequence_rows] for j in range(5)], axis=1)
    local_t = jnp.transpose(local_weight, (0, 2, 1)).reshape(5 * width, width)
    d_hidden = jnp.dot(cot_all, local_t, preferred_element_type=jnp.float32)
    middle_gradient = gelu_pull(d_hidden)[0].astype(jnp.bfloat16)
    grad_local = lax.psum_scatter(
        transposed_term(hid_all, cotangent, scale), "seq", scatter_dimension=0, tiled=True
    )
    dilated_t = jnp.transpose(dilated_weight, (0, 2, 1))
    first_part = jnp.dot(middle_gradient, dilated_t[0], preferred_element_type=jnp.float32)
    last_part = jnp.dot(middle_gradient, dilated_t[2], preferred_element_type=jnp.float32)
    centre_part = jnp.dot(middle_gradient, dilated_t[1], preferred_element_type=jnp.float32)
    moved_first = from_behind(first_part.astype(jnp.bfloat16), "seq", -dilation_stride).astype(
        first_part.dtype
    )
    moved_last = from_behind(last_part.astype(jnp.bfloat16), "seq", dilation_stride).astype(
        last_part.dtype
    )
    d_act = moved_first + centre_part + moved_last
    grad_dilated = lax.psum_scatter(
        transposed_term(gathered_activation, middle_gradient, scale),
        "seq",
        scatter_dimension=0,
        tiled=True,
    )
    input_grad = (cotangent.astype(jnp.float32) + pull(d_act)[0]).astype(jnp.bfloat16)
    return (block_out, input_grad, grad_dilated, grad_local)


def gelu_and_slope(u):
    t = jnp.tanh(GELU_A * (u + GELU_B * (u * u * u)))
    half = 0.5 * (1.0 + t)
    slope = half + 0.5 * u * (1.0 - t * t) * (GELU_A * (1.0 + 3.0 * GELU_B * (u * u)))
    return u * half, slope


def dot(x, w):
    return jnp.dot(x, w, preferred_element_type=F32)


def dot_t(x, w):
    return lax.dot_general(x, w, (((1,), (1,)), ((), ())), preferred_element_type=F32)


def bit_of(index, bit):
    return lax.rem(lax.div(index, bit), 2)


def across(index, bit):
    return index + bit - 2 * bit * bit_of(index, bit)


class HalvingSum:
    def __init__(self, me, order, rows, acc, stage, recv, out, send_sem, recv_sem, scale):
        self.me, self.order, self.rows, self.acc = me, order, rows, acc
        self.stage, self.recv, self.out = stage, recv, out
        self.send_sem, self.recv_sem, self.scale = send_sem, recv_sem, scale
        self.base = [0]
        for k in range(len(order)):
            self.base.append(self.base[-1] + 2 ** (len(order) - 1 - k))

    def combos(self, k):
        return list(itertools.product((1, 0), repeat=len(self.order) - 1 - k))

    def copy(self, k, slot):
        s = self.base[k] + slot
        return pltpu.make_async_remote_copy(
            src_ref=self.stage.at[s],
            dst_ref=self.recv.at[s],
            send_sem=self.send_sem.at[s],
            recv_sem=self.recv_sem.at[s],
            device_id={"seq": across(self.me, self.order[k])},
            device_id_type=MESH,
        )

    def block(self, flips):
        index = 0
        for bit, flip in zip(self.order, flips):
            mine = bit_of(self.me, bit)
            index = index + bit * (1 - mine if flip else mine)
        return pl.ds(pl.multiple_of(index * self.rows, 16), self.rows)

    def begin(self):
        for slot, rel in enumerate(self.combos(0)):
            self.stage[slot] = self.acc[self.block((1,) + rel), :].astype(BF16)
            self.copy(0, slot).start()

    def step(self, k):
        for slot, rel in enumerate(self.combos(k)):
            self.copy(k, slot).wait_recv()
            block = self.block((0,) * (k + 1) + rel)
            total = self.acc[block, :] + self.recv[self.base[k] + slot].astype(F32)
            if not rel:
                self.out[...] = total * self.scale
            elif rel[0]:
                later = self.combos(k + 1).index(rel[1:])
                self.stage[self.base[k + 1] + later] = total.astype(BF16)
                self.copy(k + 1, later).start()
            else:
                self.acc[block, :] = total

    def finish(self):
        for k in range(len(self.order)):
            for slot in range(len(self.combos(k))):
                self.copy(k, slot).wait_send()


def fused_kernel(
    devices, stride, scale,
    x_ref, gain_ref, dw_hbm, lw_hbm, cot_ref,
    bo_hbm, ig_hbm, gd_ref, gl_ref,
    dw_ref, lw_ref, bo_ref, ig_ref, own_sem,
    act, act_in, act_t, act_in_t, cotp, hidp, cots, d_hid, slope_in, hid_t, dmid, dmid_in,
    acc_l, acc_d, stage_l, recv_l, stage_d, recv_d,
    act_ss, act_rs, dm_ss, dm_rs, halo_ss, halo_rs, l_ss, l_rs, d_ss, d_rs,
):
    rows, width = x_ref.shape
    chunks = rows // CHUNK
    me = lax.axis_index("seq")
    upper = lax.div(me, stride)
    far = across(me, stride)
    tap_in = 2 - 2 * upper
    tap_out = 2 * upper
    has_left, has_right = me > 0, me < devices - 1
    left, right = jnp.maximum(me - 1, 0), jnp.minimum(me + 1, devices - 1)
    bits = [1 << i for i in range(devices.bit_length() - 1)]

    barrier = pltpu.get_barrier_semaphore()
    lw_in = pltpu.make_async_copy(lw_hbm, lw_ref, own_sem.at[0])
    dw_in = pltpu.make_async_copy(dw_hbm, dw_ref, own_sem.at[1])
    bo_out = pltpu.make_async_copy(bo_ref, bo_hbm, own_sem.at[2])
    ig_out = pltpu.make_async_copy(ig_ref, ig_hbm, own_sem.at[3])
    for own in (lw_in, dw_in):
        own.start()
    for bit in bits:
        pl.semaphore_signal(barrier, inc=1, device_id={"seq": across(me, bit)}, device_id_type=MESH)

    @pl.when(has_left)
    def _():
        pl.semaphore_signal(barrier, inc=1, device_id={"seq": left}, device_id_type=MESH)

    @pl.when(has_right)
    def _():
        pl.semaphore_signal(barrier, inc=1, device_id={"seq": right}, device_id_type=MESH)

    def chunk(c):
        return pl.ds(pl.multiple_of(c * CHUNK, CHUNK), CHUNK)

    def padded_chunk(c):
        return pl.ds(pl.multiple_of(PAD + c * CHUNK, PAD), CHUNK)

    def moved(src, dst, ss, rs, c):
        return pltpu.make_async_remote_copy(
            src_ref=src.at[chunk(c)], dst_ref=dst.at[chunk(c)],
            send_sem=ss.at[c], recv_sem=rs.at[c],
            device_id={"seq": far}, device_id_type=MESH,
        )

    def to_right(buf, k):
        return pltpu.make_async_remote_copy(
            src_ref=buf.at[pl.ds(rows, PAD)], dst_ref=buf.at[pl.ds(0, PAD)],
            send_sem=halo_ss.at[k], recv_sem=halo_rs.at[k],
            device_id={"seq": right}, device_id_type=MESH,
        )

    def to_left(buf, k):
        return pltpu.make_async_remote_copy(
            src_ref=buf.at[pl.ds(PAD, PAD)], dst_ref=buf.at[pl.ds(rows + PAD, PAD)],
            send_sem=halo_ss.at[k], recv_sem=halo_rs.at[k],
            device_id={"seq": left}, device_id_type=MESH,
        )

    def halo_start(buf, k):
        @pl.when(has_right)
        def _():
            to_right(buf, k).start()

        @pl.when(has_left)
        def _():
            to_left(buf, k + 1).start()

    def halo_wait(buf, k):
        @pl.when(has_right)
        def _():
            to_right(buf, k).wait_send()
            to_left(buf, k + 1).wait_recv()

        @pl.when(has_left)
        def _():
            to_left(buf, k + 1).wait_send()
            to_right(buf, k).wait_recv()

    @pl.when(jnp.logical_not(has_left))
    def _():
        cotp[0:PAD, :] = jnp.zeros((PAD, width), BF16)
        hidp[0:PAD, :] = jnp.zeros((PAD, width), BF16)

    @pl.when(jnp.logical_not(has_right))
    def _():
        cotp[rows + PAD : rows + 2 * PAD, :] = jnp.zeros((PAD, width), BF16)
        hidp[rows + PAD : rows + 2 * PAD, :] = jnp.zeros((PAD, width), BF16)

    def prepare_chunk(c):
        v = x_ref[chunk(c), :].astype(F32)
        rstd = lax.rsqrt(jnp.mean(v * v, axis=-1, keepdims=True) + 1e-06)
        a, slope = gelu_and_slope(v * rstd * gain_ref[...])
        act[chunk(c), :] = a.astype(BF16)
        slope_in[chunk(c), :] = slope * gain_ref[...]

    cotp[PAD : rows + PAD, :] = cot_ref[...]
    prepare_chunk(0)
    pl.semaphore_wait(
        barrier, len(bits) + has_left.astype(jnp.int32) + has_right.astype(jnp.int32)
    )
    halo_start(cotp, 0)
    moved(act, act_in, act_ss, act_rs, 0).start()

    def prepare_and_send(c, _):
        prepare_chunk(c)
        moved(act, act_in, act_ss, act_rs, c).start()
        return 0

    lax.fori_loop(1, chunks, prepare_and_send, 0)
    lw_in.wait()
    dw_in.wait()
    halo_wait(cotp, 0)

    def cot_chunk(c, _):
        window = cotp[pl.ds(pl.multiple_of(c * CHUNK, CHUNK), CHUNK + 2 * PAD), :].astype(F32)
        total = jnp.zeros((CHUNK, width), F32)
        for j in range(5):
            shifted = window[PAD + 2 - j : PAD + 2 - j + CHUNK].astype(BF16)
            cots[j, chunk(c), :] = shifted
            total = total + dot_t(shifted, lw_ref[j])
        d_hid[chunk(c), :] = total
        act_t[:, chunk(c)] = act[chunk(c), :].astype(F32).T.astype(BF16)
        return 0

    lax.fori_loop(0, chunks, cot_chunk, 0)

    def middle_chunk(c, _):
        moved(act, act_in, act_ss, act_rs, c).wait_recv()
        other = act_in[chunk(c), :]
        mid = dot(act[chunk(c), :], dw_ref[1]) + dot(other, dw_ref[tap_in])
        hid, slope = gelu_and_slope(mid)
        dm = (d_hid[chunk(c), :] * slope).astype(BF16)
        dmid[chunk(c), :] = dm

        @pl.when(c >= LAG)
        def _():
            moved(dmid, dmid_in, dm_ss, dm_rs, c - LAG).start()

        hid = hid.astype(BF16)
        hidp[padded_chunk(c), :] = hid
        hid_t[:, chunk(c)] = hid.astype(F32).T.astype(BF16)
        act_in_t[:, chunk(c)] = other.astype(F32).T.astype(BF16)
        return 0

    lax.fori_loop(0, chunks, middle_chunk, 0)
    halo_start(hidp, 2)

    def late_send(c, _):
        moved(dmid, dmid_in, dm_ss, dm_rs, c).start()
        return 0


    sum_l = HalvingSum(
        me, bits, gl_ref.shape[0], acc_l, stage_l, recv_l, gl_ref, l_ss, l_rs, scale
    )
    d_order = [bits[0], bits[2], bits[1]] + bits[3:]
    sum_d = HalvingSum(
        me, d_order, gd_ref.shape[0], acc_d, stage_d, recv_d, gd_ref, d_ss, d_rs, scale
    )

    def local_tap(j, _):
        acc_l[pl.ds(pl.multiple_of(j * width, width), width), :] = dot(hid_t[...], cots[j])
        return 0

    lax.fori_loop(0, 5, local_tap, 0)
    lax.fori_loop(chunks - LAG, chunks - 2, late_send, 0)
    sum_l.begin()
    acc_d[width : 2 * width, :] = dot(act_t[...], dmid[...])
    acc_d[pl.ds(pl.multiple_of(tap_in * width, width), width), :] = dot(act_in_t[...], dmid[...])
    acc_d[pl.ds(pl.multiple_of(tap_out * width, width), width), :] = jnp.zeros((width, width), F32)
    sum_d.begin()
    sum_l.step(0)
    sum_d.step(0)
    lax.fori_loop(chunks - 2, chunks, late_send, 0)

    for k in range(1, len(bits) - 1):
        sum_l.step(k)
        sum_d.step(k)

    halo_wait(hidp, 2)

    def out_chunk(c, _):
        window = hidp[pl.ds(pl.multiple_of(c * CHUNK, CHUNK), CHUNK + 2 * PAD), :].astype(F32)
        total = x_ref[chunk(c), :].astype(F32)
        for j in range(5):
            total = total + dot(window[PAD - 2 + j : PAD - 2 + j + CHUNK].astype(BF16), lw_ref[j])
        bo_ref[chunk(c), :] = total.astype(BF16)
        return 0

    lax.fori_loop(0, chunks, out_chunk, 0)
    bo_out.start()

    def grad_chunk(c, _):
        moved(dmid, dmid_in, dm_ss, dm_rs, c).wait_recv()
        d_act = dot_t(dmid[chunk(c), :], dw_ref[1]) + dot_t(dmid_in[chunk(c), :], dw_ref[tap_out])
        v = x_ref[chunk(c), :].astype(F32)
        rstd = lax.rsqrt(jnp.mean(v * v, axis=-1, keepdims=True) + 1e-06)
        du = d_act * slope_in[chunk(c), :]
        unit = v * rstd
        dv = rstd * (du - unit * jnp.mean(du * unit, axis=-1, keepdims=True))
        ig_ref[chunk(c), :] = (cotp[padded_chunk(c), :].astype(F32) + dv).astype(BF16)
        return 0

    lax.fori_loop(0, chunks, grad_chunk, 0)
    ig_out.start()
    sum_l.step(len(bits) - 1)
    sum_d.step(len(bits) - 1)

    def sent(c, _):
        moved(act, act_in, act_ss, act_rs, c).wait_send()
        moved(dmid, dmid_in, dm_ss, dm_rs, c).wait_send()
        return 0

    lax.fori_loop(0, chunks, sent, 0)
    bo_out.wait()
    ig_out.wait()
    sum_l.finish()
    sum_d.finish()


def handing_kernel(*refs):
    count = len(refs) // 3
    sources, targets, held, sems = refs[:count], refs[count : 2 * count], refs[2 * count : -1], refs[-1]
    ins = [pltpu.make_async_copy(sources[i], held[i], sems.at[0, i]) for i in range(count)]
    outs = [pltpu.make_async_copy(held[i], targets[i], sems.at[1, i]) for i in range(count)]
    for copy in ins:
        copy.start()
    for i in range(count):
        ins[i].wait()
        outs[i].start()
    for copy in outs:
        copy.wait()


def handed_on(results):
    left_out = pl.BlockSpec(memory_space=pl.ANY)
    return pl.pallas_call(
        handing_kernel,
        out_shape=tuple(jax.ShapeDtypeStruct(r.shape, r.dtype) for r in results),
        in_specs=[left_out] * len(results),
        out_specs=(left_out,) * len(results),
        scratch_shapes=[pltpu.VMEM(r.shape, r.dtype) for r in results]
        + [pltpu.SemaphoreType.DMA((2, len(results)))],
    )(*results)


def paired(devices, inputs, norm_gain, dilated_weight, local_weight, cotangent):
    rows, width = inputs.shape
    stride = DILATION_BINS // rows
    scale = 1.0 / math.sqrt(rows * devices)
    chunks = rows // CHUNK
    rows_d, rows_l = 3 * width // devices, 5 * width // devices
    vmem = pltpu.VMEM
    dma = pltpu.SemaphoreType.DMA
    whole = pl.BlockSpec(memory_space=pltpu.VMEM)
    left_out = pl.BlockSpec(memory_space=pl.ANY)
    flops = 2 * rows * width * width * (5 * 3 + 2 * 3)
    results = pl.pallas_call(
        functools.partial(fused_kernel, devices, stride, scale),
        out_shape=(
            jax.ShapeDtypeStruct((rows, width), BF16),
            jax.ShapeDtypeStruct((rows, width), BF16),
            jax.ShapeDtypeStruct((rows_d, width), F32),
            jax.ShapeDtypeStruct((rows_l, width), F32),
        ),
        in_specs=[whole, whole, left_out, left_out, whole],
        out_specs=(left_out, left_out, whole, whole),
        scratch_shapes=[
            vmem((3, width, width), BF16),
            vmem((5, width, width), BF16),
            vmem((rows, width), BF16),
            vmem((rows, width), BF16),
            dma((4,)),
            vmem((rows, width), BF16),
            vmem((rows, width), BF16),
            vmem((width, rows), BF16),
            vmem((width, rows), BF16),
            vmem((rows + 2 * PAD, width), BF16),
            vmem((rows + 2 * PAD, width), BF16),
            vmem((5, rows, width), BF16),
            vmem((rows, width), F32),
            vmem((rows, width), F32),
            vmem((width, rows), BF16),
            vmem((rows, width), BF16),
            vmem((rows, width), BF16),
            vmem((5 * width, width), F32),
            vmem((3 * width, width), F32),
            vmem((devices - 1, rows_l, width), BF16),
            vmem((devices - 1, rows_l, width), BF16),
            vmem((devices - 1, rows_d, width), BF16),
            vmem((devices - 1, rows_d, width), BF16),
            dma((chunks,)), dma((chunks,)), dma((chunks,)), dma((chunks,)),
            dma((4,)), dma((4,)),
            dma((devices - 1,)), dma((devices - 1,)), dma((devices - 1,)), dma((devices - 1,)),
        ],
        compiler_params=pltpu.CompilerParams(
            collective_id=0, has_side_effects=True, vmem_limit_bytes=58 * 2**20
        ),
        cost_estimate=pl.CostEstimate(
            flops=flops, bytes_accessed=12 * 2**20, transcendentals=2 * rows * width
        ),
    )(inputs, norm_gain.reshape(1, width), dilated_weight, local_weight, cotangent)
    return handed_on(results)


def pairs_up(devices, rows, width):
    return (
        devices >= 8
        and devices & (devices - 1) == 0
        and devices * rows == 2 * DILATION_BINS
        and rows % CHUNK == 0
        and width % (16 * devices) == 0
    )


def solution(mesh):
    def body(inputs, norm_gain, dilated_weight, local_weight, cotangent):
        arrays = (inputs, norm_gain, dilated_weight, local_weight, cotangent)
        devices = mesh.shape["seq"]
        if pairs_up(devices, *inputs.shape):
            return paired(devices, *arrays)
        return on_device(*arrays)

    return jax.shard_map(
        body,
        mesh=mesh,
        in_specs=(P(("groups", "seq"), None), P(), P(), P(), P(("groups", "seq"), None)),
        out_specs=(
            P(("groups", "seq"), None),
            P(("groups", "seq"), None),
            P(("groups", "seq"), None),
            P(("groups", "seq"), None),
        ),
        check_vma=False,
    )
```
